32 devices in a mesh: shots: 2 (over y), lat: 4 (over z), freq: 2 (over x), sub: 2 (over core).
Axes of the slice: x: 2, y: 2, z: 4, core: 2. Of those that a mesh axis runs over, the one named last changes fastest.
Arguments:
- wavefields: float32 [4, 4, 64, 1024], P(('shots', 'freq'), None, 'lat', 'sub'), parts along dimension 0, may hold values from -6 to 6
- velocity: float32 [8, 64, 1024], P('freq', 'lat', 'sub'), may hold values from 0 to 31
- filter_table: float32 [32, 32, 9, 2], replicated, may hold values from -1 to 1
- freq_pick: int32 [2], P('freq'), may hold values from 0 to 31
- slab_order: int32 [4], replicated, may hold values from 0 to 7
Outputs:
- fields_out: float32 [4, 4, 64, 1024], P(('shots', 'freq'), None, 'lat', 'sub'), parts along dimension 0
- image: float32 [8, 64, 1024], P(('shots', 'freq'), 'lat', 'sub'), parts along dimension 0
The draws below stay inside these ranges and needn't reach their ends.
There are 2 independent parts, one for each index of `shots`. The reference program is written for one: setup_inputs(seed, part) draws one part's arguments, and reference() takes and returns one part's arrays. A program takes and returns all parts, laid end to end along the dimension named above; an argument that names none is the same for every part. Nothing has to cross between parts.
All inputs are finite; a program needn't handle non-finite values.
Results may differ from the reference program's by a relative error of at most 0.0003.
Values sent between devices are 32-bit elements; how exact they have to be, the bound alone decides.
A program may use at most 64 MiB of HBM per device.

```python
import jax
import jax.numpy as jnp
from jax import lax

DEPTHS = 4
KCHEB = 8
NBINS = 32
TABLE_FREQS = 32
STORED = 8
FREQS = 2
NX = 64
NY = 1024


def place_ends(result, stream_key, smallest, high):
    longest = result.shape.index(max(result.shape))
    spots = []
    for shift in (0, 1):
        where = [jax.random.randint(jax.random.fold_in(stream_key, axis), (), 0, length) for axis, length in enumerate(result.shape)]
        where[longest] = (where[longest] + shift) % result.shape[longest]
        spots.append(tuple(where))
    return result.at[spots[0]].set(smallest).at[spots[1]].set(high)


def steps_of(own_key, extent, split, smallest, top_value):
    def one(dim, shards_of):
        steps = jax.random.uniform(jax.random.fold_in(jax.random.fold_in(own_key, 6), dim), (shards_of,), jnp.float32, smallest / len(split), top_value / len(split))
        return jnp.repeat(jnp.exp(steps), extent[dim] // shards_of).reshape((-1,) + (1,) * (len(extent) - dim - 1))

    factor_of = one(*split[0])
    for cut in split[1:]:
        factor_of = factor_of * one(*cut)
    return factor_of


def centred(stream_key, shape, scale, reach, split=(), kind=jnp.bfloat16):
    values = jax.random.normal(stream_key, shape, jnp.float32) * scale
    if len(split) > 0:
        values = steps_of(stream_key, shape, split, -0.22, 0.18) * values
    return jnp.clip(values, min=-reach, max=reach).astype(kind)


def setup_inputs(seed: int = 0, part: int = 0) -> dict:
    arg_keys = jax.random.split(jax.random.key(seed), 6)
    part_keys = jax.random.split(jax.random.fold_in(arg_keys[5], part), 6)
    return {
        "wavefields": centred(part_keys[0], (FREQS, 4, NX, NY), 1.0, 6.0, ((0, 2), (2, 4), (3, 2)), jnp.float32),
        "velocity": jnp.clip(31.0 * jax.random.uniform(arg_keys[1], (STORED, NX, NY), jnp.float32) ** steps_of(arg_keys[1], (STORED, NX, NY), ((0, 2), (1, 4), (2, 2)), -0.2, 0.2), 0.0, 31.0),
        "filter_table": centred(arg_keys[2], (NBINS, TABLE_FREQS, KCHEB + 1, 2), 0.25, 1.0, (), jnp.float32),
        "freq_pick": jax.random.randint(arg_keys[3], (FREQS,), 0, TABLE_FREQS).astype(jnp.int32),
        "slab_order": place_ends(jax.random.randint(arg_keys[4], (DEPTHS,), 0, STORED), jax.random.fold_in(arg_keys[4], 1), 0, STORED - 1).astype(jnp.int32),
    }


def stencil(padded):
    edges = padded[:, :, 2:, 1:-1] + padded[:, :, :-2, 1:-1] + padded[:, :, 1:-1, 2:] + padded[:, :, 1:-1, :-2]
    corners = padded[:, :, 2:, 2:] + padded[:, :, 2:, :-2] + padded[:, :, :-2, 2:] + padded[:, :, :-2, :-2]
    return -0.5 * padded[:, :, 1:-1, 1:-1] + 0.25 * edges + 0.125 * corners


def operate(field):
    return stencil(jnp.pad(field, ((0, 0), (0, 0), (1, 1), (1, 1))))


def combine(pair, term):
    real_part = pair[:, 0][:, None]
    imag_part = pair[:, 1][:, None]
    turned = jnp.stack([term[:, 1], -term[:, 0], -term[:, 3], term[:, 2]], axis=1)
    return real_part * term + imag_part * turned


def reference(wavefields, velocity, filter_table, freq_pick, slab_order):
    highest = lax.Precision.HIGHEST
    onehot = (freq_pick[:, None] == jnp.arange(TABLE_FREQS, dtype=jnp.int32)[None, :]).astype(jnp.float32)
    selected = jnp.einsum("ft,btkc->bfkc", onehot, filter_table, precision=highest)
    selected = selected.reshape(NBINS, FREQS * (KCHEB + 1) * 2).T
    bin_grid = jnp.arange(NBINS, dtype=jnp.float32)[:, None]
    fields = wavefields
    images = []
    for depth_step in range(DEPTHS):
        slowness = velocity[slab_order[depth_step]]
        weights = jnp.maximum(0.0, 1.0 - jnp.abs(slowness.reshape(1, -1) - bin_grid))
        coefficients = jnp.dot(selected, weights, precision=highest, preferred_element_type=jnp.float32)
        coefficients = coefficients.reshape(FREQS, KCHEB + 1, 2, NX, NY)
        previous = fields
        summed = combine(coefficients[:, 0], previous)
        current = operate(previous)
        summed = summed + combine(coefficients[:, 1], current)
        for order in range(2, KCHEB + 1):
            following = 2.0 * operate(current) - previous
            previous, current = current, following
            summed = summed + combine(coefficients[:, order], current)
        fields = summed
        images.append(jnp.sum(fields[:, 0] * fields[:, 2] + fields[:, 1] * fields[:, 3], axis=0))
    return fields, jnp.stack(images)
```

```python
import functools

import jax
import jax.numpy as jnp
from jax import lax
from jax.experimental import pallas as pl
from jax.experimental.pallas import tpu as pltpu
from jax.sharding import PartitionSpec as P

KCHEB = 8
ORDERS = KCHEB + 1
HALO = 8
LANES = 128
MESH = pl.DeviceIdType.MESH


def kernel(sizes, wave_ref, vel_ref, tab_ref, slab_ref, out_ref, image_ref,
           fields, slots, coef, partial, arrived,
           halo_send, halo_recv, vel_send, vel_recv, img_send, img_recv):
    lats, freqs, bins = sizes
    depths = slab_ref.shape[0]
    slab_size, rows, cols = vel_ref.shape
    tiles = cols // LANES
    per = image_ref.shape[0]
    tall = rows + 2 * HALO
    lat = lax.axis_index("lat")
    sub = lax.axis_index("sub")
    freq = lax.axis_index("freq")
    has_up = lat > 0
    has_down = lat < lats - 1
    other = 1 - sub
    edge_tile = (tiles - 1) * (1 - sub)

    barrier = pltpu.get_barrier_semaphore()

    def greet(target):
        pl.semaphore_signal(barrier, inc=1, device_id=target, device_id_type=MESH)

    greet({"sub": other})
    for step in range(1, freqs):
        greet({"freq": lax.rem(freq + step, freqs)})

    @pl.when(has_up)
    def _():
        greet({"lat": lat - 1})
        greet({"lat": lat - 1, "sub": other})

    @pl.when(has_down)
    def _():
        greet({"lat": lat + 1})
        greet({"lat": lat + 1, "sub": other})

    pl.semaphore_wait(
        barrier, freqs + jnp.where(has_up, 2, 0) + jnp.where(has_down, 2, 0)
    )

    def vel_copy(d, source, target):
        return pltpu.make_async_remote_copy(
            src_ref=slots.at[d, source],
            dst_ref=slots.at[d, source],
            send_sem=vel_send.at[d, target],
            recv_sem=vel_recv.at[d, source],
            device_id={"freq": target},
            device_id_type=MESH,
        )

    def halo_copy(d, pair, way):
        src_rows = {0: HALO, 1: rows, 2: HALO, 3: HALO, 4: rows}[way]
        dst_rows = {0: HALO + rows, 1: 0, 2: HALO, 3: HALO + rows, 4: 0}[way]
        count = rows if way == 2 else HALO
        src_tiles, dst_tiles = (
            (pl.ds(0, tiles), pl.ds(0, tiles))
            if way < 2
            else (pl.ds(edge_tile, 1), pl.ds(tiles, 1))
        )
        target = {}
        if way in (0, 3):
            target["lat"] = lat - 1
        if way in (1, 4):
            target["lat"] = lat + 1
        if way >= 2:
            target["sub"] = other
        parts = pl.ds(2 * pair, 2)
        return pltpu.make_async_remote_copy(
            src_ref=fields.at[d, parts, src_tiles, pl.ds(src_rows, count)],
            dst_ref=fields.at[d, parts, dst_tiles, pl.ds(dst_rows, count)],
            send_sem=halo_send.at[d, pair, way],
            recv_sem=halo_recv.at[d, pair, way],
            device_id=target,
            device_id_type=MESH,
        )

    def send_halo(d, pair):
        @pl.when(has_up)
        def _():
            halo_copy(d, pair, 0).start()
            halo_copy(d, pair, 3).start()

        @pl.when(has_down)
        def _():
            halo_copy(d, pair, 1).start()
            halo_copy(d, pair, 4).start()

        halo_copy(d, pair, 2).start()

    def wait_halo(d, pair):
        halo_copy(d, pair, 2).wait_recv()

        @pl.when(has_down)
        def _():
            halo_copy(d, pair, 0).wait_recv()
            halo_copy(d, pair, 3).wait_recv()

        @pl.when(has_up)
        def _():
            halo_copy(d, pair, 1).wait_recv()
            halo_copy(d, pair, 4).wait_recv()

    def wait_halo_sent(d, pair):
        @pl.when(has_up)
        def _():
            halo_copy(d, pair, 0).wait_send()
            halo_copy(d, pair, 3).wait_send()

        @pl.when(has_down)
        def _():
            halo_copy(d, pair, 1).wait_send()
            halo_copy(d, pair, 4).wait_send()

        halo_copy(d, pair, 2).wait_send()

    for pair in range(2):
        for part in (2 * pair, 2 * pair + 1):
            for t in range(tiles):
                fields[0, part, t, pl.ds(HALO, rows)] = wave_ref[0, part, :, t * LANES:(t + 1) * LANES]
        send_halo(0, pair)
        for d in range(depths) if pair == 0 else ():
            slots[d, freq] = vel_ref[slab_ref[d] % slab_size]
            for step in range(1, freqs):
                vel_copy(d, freq, lax.rem(freq + step, freqs)).start()

    lane = lax.broadcasted_iota(jnp.int32, (tall, LANES), 1)
    row = lax.broadcasted_iota(jnp.int32, (tall, LANES), 0)
    row_low = jnp.where(has_up, 0, HALO)
    row_high = jnp.where(has_down, tall, tall - HALO)
    row_mask = (row >= row_low) & (row < row_high)
    lane_low = jnp.where(sub == 0, 0, LANES // 2)
    halo_mask = row_mask & (lane >= lane_low) & (lane < lane_low + LANES // 2)
    first_lane = lane == 0
    last_lane = lane == LANES - 1

    def make_coefficients(d):
        for step in range(1, freqs):
            source = lax.rem(freq + step, freqs)
            vel_copy(d, source, source).wait_recv()
        owner = slab_ref[d] // slab_size
        for t in range(tiles):
            for r in range(0, rows, 8):
                v = jnp.zeros((8, LANES), jnp.float32)
                for source in range(freqs):
                    block = slots[d, source, r:r + 8, t * LANES:(t + 1) * LANES]
                    v = jnp.where(owner == source, block, v)
                base = jnp.floor(v)
                upper = v - base
                lower = 1.0 - upper
                index = jnp.clip(base.astype(jnp.int32), 0, bins - 1)
                index_next = jnp.minimum(index + 1, bins - 1)
                for j in range(ORDERS * 2):
                    start = j * bins
                    window, shift = start // LANES, start % LANES
                    table = jnp.broadcast_to(
                        tab_ref[0:1, window * LANES:(window + 1) * LANES], (8, LANES)
                    )
                    low = jnp.take_along_axis(table, index + shift, axis=1, mode="promise_in_bounds")
                    high = jnp.take_along_axis(table, index_next + shift, axis=1, mode="promise_in_bounds")
                    coef[j, t, pl.ds(r, 8)] = low * lower + high * upper

    def smooth(xs):
        ys = []
        for x in xs:
            w = x + pltpu.roll(x, tall - 1, 0)
            ys.append(w + pltpu.roll(w, 1, 0))
        n = len(ys)
        left = [pltpu.roll(y, LANES - 1, 1) for y in ys]
        ws = [ys[t] + jnp.where(last_lane, left[(t + 1) % n], left[t]) for t in range(n)]
        right = [pltpu.roll(w, 1, 1) for w in ws]
        return [ws[t] + jnp.where(first_lane, right[t - 1], right[t]) for t in range(n)]

    def masked(xs):
        return [jnp.where(row_mask if t < tiles else halo_mask, x, 0.0) for t, x in enumerate(xs)]

    def propagate(d, pair):
        sign = 1.0 if pair == 0 else -1.0
        now = [
            masked([fields[d, 2 * pair + part, t] for t in range(tiles + 1)]) for part in range(2)
        ]
        before = None
        total = [[None] * tiles for _ in range(2)]
        for k in range(ORDERS):
            if k > 0:
                new = []
                for part in range(2):
                    sums = smooth(now[part])
                    if k == 1:
                        xs = [0.125 * s - x for s, x in zip(sums, now[part])]
                    else:
                        xs = [
                            0.25 * s - (2.0 * x + y)
                            for s, x, y in zip(sums, now[part], before[part])
                        ]
                    new.append(masked(xs) if k < KCHEB else xs)
                before, now = now, new
            for t in range(tiles):
                a = coef[2 * k, t]
                b = coef[2 * k + 1, t]
                p = now[0][t][HALO:HALO + rows]
                q = now[1][t][HALO:HALO + rows]
                if pair == 0:
                    add0, add1 = a * p + b * q, a * q - b * p
                else:
                    add0, add1 = a * p - b * q, a * q + b * p
                total[0][t] = add0 if k == 0 else total[0][t] + add0
                total[1][t] = add1 if k == 0 else total[1][t] + add1
        for part in range(2):
            for t in range(tiles):
                fields[d + 1, 2 * pair + part, t, pl.ds(HALO, rows)] = total[part][t]

    def image_copy(d, source, owner):
        return pltpu.make_async_remote_copy(
            src_ref=partial.at[d],
            dst_ref=arrived.at[d, source],
            send_sem=img_send.at[d],
            recv_sem=img_recv.at[d, source],
            device_id={"freq": owner},
            device_id_type=MESH,
        )

    make_coefficients(0)

    def depth_step(d, carry):
        for pair in range(2):
            wait_halo(d, pair)
            propagate(d, pair)

            @pl.when(d < depths - 1)
            def _():
                send_halo(d + 1, pair)

        for t in range(tiles):
            u = [fields[d + 1, part, t, pl.ds(HALO, rows)] for part in range(4)]
            partial[d, :, t * LANES:(t + 1) * LANES] = u[0] * u[2] + u[1] * u[3]
        owner = d // per

        @pl.when(owner != freq)
        def _():
            image_copy(d, freq, owner).start()

        @pl.when(d < depths - 1)
        def _():
            make_coefficients(d + 1)

        return carry

    lax.fori_loop(0, depths, depth_step, 0)

    for part in range(4):
        for t in range(tiles):
            out_ref[0, part, :, t * LANES:(t + 1) * LANES] = fields[depths, part, t, pl.ds(HALO, rows)]

    for i in range(per):
        d = freq * per + i
        total = partial[d]
        for step in range(1, freqs):
            source = lax.rem(freq + step, freqs)
            image_copy(d, source, source).wait_recv()
            total = total + arrived[d, source]
        image_ref[i] = total

    for d in range(depths):
        for pair in range(2):
            wait_halo_sent(d, pair)
        for step in range(1, freqs):
            vel_copy(d, freq, lax.rem(freq + step, freqs)).wait_send()

        @pl.when(d // per != freq)
        def _():
            image_copy(d, freq, d // per).wait_send()


def body(sizes, wavefields, velocity, filter_table, freq_pick, slab_order):
    lats, freqs = sizes
    depths = slab_order.shape[0]
    _, parts, rows, cols = wavefields.shape
    tiles = cols // LANES
    bins = filter_table.shape[0]
    per = depths // freqs
    table = lax.dynamic_index_in_dim(filter_table, freq_pick[0], 1, keepdims=False)
    table = jnp.transpose(table, (1, 2, 0)).reshape(1, ORDERS * 2 * bins)
    wide = -(-table.shape[1] // LANES) * LANES
    table = jnp.pad(table, ((0, 0), (0, wide - table.shape[1])))
    vmem = pl.BlockSpec(memory_space=pltpu.VMEM)
    return pl.pallas_call(
        functools.partial(kernel, (lats, freqs, bins)),
        out_shape=(
            jax.ShapeDtypeStruct(wavefields.shape, jnp.float32),
            jax.ShapeDtypeStruct((per, rows, cols), jnp.float32),
        ),
        in_specs=[vmem, vmem, vmem, pl.BlockSpec(memory_space=pltpu.SMEM)],
        out_specs=(vmem, vmem),
        scratch_shapes=[
            pltpu.VMEM((depths + 1, parts, tiles + 1, rows + 2 * HALO, LANES), jnp.float32),
            pltpu.VMEM((depths, freqs, rows, cols), jnp.float32),
            pltpu.VMEM((ORDERS * 2, tiles, rows, LANES), jnp.float32),
            pltpu.VMEM((depths, rows, cols), jnp.float32),
            pltpu.VMEM((depths, freqs, rows, cols), jnp.float32),
            pltpu.SemaphoreType.DMA((depths, 2, 5)),
            pltpu.SemaphoreType.DMA((depths, 2, 5)),
            pltpu.SemaphoreType.DMA((depths, freqs)),
            pltpu.SemaphoreType.DMA((depths, freqs)),
            pltpu.SemaphoreType.DMA((depths,)),
            pltpu.SemaphoreType.DMA((depths, freqs)),
        ],
        compiler_params=pltpu.CompilerParams(
            collective_id=0, has_side_effects=True, vmem_limit_bytes=32 * 1024 * 1024
        ),
    )(wavefields, velocity, table, slab_order)


def solution(mesh):
    sizes = (mesh.shape["lat"], mesh.shape["freq"])
    return jax.shard_map(
        functools.partial(body, sizes),
        mesh=mesh,
        in_specs=(
            P(("shots", "freq"), None, "lat", "sub"),
            P("freq", "lat", "sub"),
            P(),
            P("freq"),
            P(),
        ),
        out_specs=(P(("shots", "freq"), None, "lat", "sub"), P(("shots", "freq"), "lat", "sub")),
        check_vma=False,
    )
```

```python
import functools

import jax
import jax.numpy as jnp
from jax import lax
from jax.experimental import pallas as pl
from jax.experimental.pallas import tpu as pltpu
from jax.sharding import PartitionSpec as P

KCHEB = 8
ORDERS = KCHEB + 1
HALO = 8
LANES = 128
MESH = pl.DeviceIdType.MESH


def kernel(sizes, wave_ref, vel_ref, tab_ref, slab_ref, out_ref, image_ref,
           fields, slots, coef, partial, arrived, work,
           halo_send, halo_recv, vel_send, vel_recv, img_send, img_recv):
    lats, freqs, bins = sizes
    depths = slab_ref.shape[0]
    slab_size, rows, cols = vel_ref.shape
    tiles = cols // LANES
    per = image_ref.shape[0]
    tall = rows + 2 * HALO
    lat = lax.axis_index("lat")
    sub = lax.axis_index("sub")
    freq = lax.axis_index("freq")
    has_up = lat > 0
    has_down = lat < lats - 1
    other = 1 - sub
    edge_tile = (tiles - 1) * (1 - sub)

    barrier = pltpu.get_barrier_semaphore()

    def greet(target):
        pl.semaphore_signal(barrier, inc=1, device_id=target, device_id_type=MESH)

    greet({"sub": other})
    for step in range(1, freqs):
        greet({"freq": lax.rem(freq + step, freqs)})

    @pl.when(has_up)
    def _():
        greet({"lat": lat - 1})
        greet({"lat": lat - 1, "sub": other})

    @pl.when(has_down)
    def _():
        greet({"lat": lat + 1})
        greet({"lat": lat + 1, "sub": other})

    pl.semaphore_wait(
        barrier, freqs + jnp.where(has_up, 2, 0) + jnp.where(has_down, 2, 0)
    )

    def vel_copy(d, source, target):
        return pltpu.make_async_remote_copy(
            src_ref=slots.at[d, source],
            dst_ref=slots.at[d, source],
            send_sem=vel_send.at[d, target],
            recv_sem=vel_recv.at[d, source],
            device_id={"freq": target},
            device_id_type=MESH,
        )

    def halo_copy(d, pair, way):
        src_rows = {0: HALO, 1: rows, 2: HALO, 3: HALO, 4: rows}[way]
        dst_rows = {0: HALO + rows, 1: 0, 2: HALO, 3: HALO + rows, 4: 0}[way]
        count = rows if way == 2 else HALO
        src_tiles, dst_tiles = (
            (pl.ds(0, tiles), pl.ds(0, tiles))
            if way < 2
            else (pl.ds(edge_tile, 1), pl.ds(tiles, 1))
        )
        target = {}
        if way in (0, 3):
            target["lat"] = lat - 1
        if way in (1, 4):
            target["lat"] = lat + 1
        if way >= 2:
            target["sub"] = other
        parts = pl.ds(2 * pair, 2)
        return pltpu.make_async_remote_copy(
            src_ref=fields.at[d, parts, src_tiles, pl.ds(src_rows, count)],
            dst_ref=fields.at[d, parts, dst_tiles, pl.ds(dst_rows, count)],
            send_sem=halo_send.at[d, pair, way],
            recv_sem=halo_recv.at[d, pair, way],
            device_id=target,
            device_id_type=MESH,
        )

    def send_halo(d, pair):
        @pl.when(has_up)
        def _():
            halo_copy(d, pair, 0).start()
            halo_copy(d, pair, 3).start()

        @pl.when(has_down)
        def _():
            halo_copy(d, pair, 1).start()
            halo_copy(d, pair, 4).start()

        halo_copy(d, pair, 2).start()

    def wait_halo(d, pair):
        halo_copy(d, pair, 2).wait_recv()

        @pl.when(has_down)
        def _():
            halo_copy(d, pair, 0).wait_recv()
            halo_copy(d, pair, 3).wait_recv()

        @pl.when(has_up)
        def _():
            halo_copy(d, pair, 1).wait_recv()
            halo_copy(d, pair, 4).wait_recv()

    def wait_halo_sent(d, pair):
        @pl.when(has_up)
        def _():
            halo_copy(d, pair, 0).wait_send()
            halo_copy(d, pair, 3).wait_send()

        @pl.when(has_down)
        def _():
            halo_copy(d, pair, 1).wait_send()
            halo_copy(d, pair, 4).wait_send()

        halo_copy(d, pair, 2).wait_send()

    for pair in range(2):
        for part in (2 * pair, 2 * pair + 1):
            for t in range(tiles):
                fields[0, part, t, pl.ds(HALO, rows)] = wave_ref[0, part, :, t * LANES:(t + 1) * LANES]
        send_halo(0, pair)
        for d in range(depths) if pair == 0 else ():
            slots[d, freq] = vel_ref[slab_ref[d] % slab_size]
            for step in range(1, freqs):
                vel_copy(d, freq, lax.rem(freq + step, freqs)).start()

    lane = lax.broadcasted_iota(jnp.int32, (tall, LANES), 1)
    row = lax.broadcasted_iota(jnp.int32, (tall, LANES), 0)
    row_low = jnp.where(has_up, 0, HALO)
    row_high = jnp.where(has_down, tall, tall - HALO)
    row_mask = (row >= row_low) & (row < row_high)
    lane_low = jnp.where(sub == 0, 0, LANES // 2)
    halo_mask = row_mask & (lane >= lane_low) & (lane < lane_low + LANES // 2)
    first_lane = lane == 0
    last_lane = lane == LANES - 1

    def make_coefficients(d):
        for step in range(1, freqs):
            source = lax.rem(freq + step, freqs)
            vel_copy(d, source, source).wait_recv()
        owner = slab_ref[d] // slab_size
        for t in range(tiles):
            for r in range(0, rows, 8):
                v = jnp.zeros((8, LANES), jnp.float32)
                for source in range(freqs):
                    block = slots[d, source, r:r + 8, t * LANES:(t + 1) * LANES]
                    v = jnp.where(owner == source, block, v)
                base = jnp.floor(v)
                upper = v - base
                lower = 1.0 - upper
                index = jnp.clip(base.astype(jnp.int32), 0, bins - 1)
                index_next = jnp.minimum(index + 1, bins - 1)
                for j in range(ORDERS * 2):
                    start = j * bins
                    window, shift = start // LANES, start % LANES
                    table = jnp.broadcast_to(
                        tab_ref[0:1, window * LANES:(window + 1) * LANES], (8, LANES)
                    )
                    low = jnp.take_along_axis(table, index + shift, axis=1, mode="promise_in_bounds")
                    high = jnp.take_along_axis(table, index_next + shift, axis=1, mode="promise_in_bounds")
                    coef[j, t, pl.ds(r, 8)] = low * lower + high * upper

    def smooth(xs, k, parity, pair, part):
        shift = parity * 8
        ys = []
        for t, x in enumerate(xs):
            line = work.at[k % 2, 2 * pair + part, t]
            line[pl.ds(pl.multiple_of(shift + 8, 8), tall)] = x
            ys.append(line[pl.ds(shift + 7, tall)] + line[pl.ds(shift + 9, tall)] + (x + x))
        n = len(ys)
        left = [pltpu.roll(y, LANES - 1, 1) for y in ys]
        right = [pltpu.roll(y, 1, 1) for y in ys]
        return [
            (ys[t] + ys[t])
            + jnp.where(last_lane, left[(t + 1) % n], left[t])
            + jnp.where(first_lane, right[t - 1], right[t])
            for t in range(n)
        ]

    def masked(xs):
        return [jnp.where(row_mask if t < tiles else halo_mask, x, 0.0) for t, x in enumerate(xs)]

    def propagate(d, pair):
        sign = 1.0 if pair == 0 else -1.0
        now = [
            masked([fields[d, 2 * pair + part, t] for t in range(tiles + 1)]) for part in range(2)
        ]
        before = None
        total = [[None] * tiles for _ in range(2)]
        for k in range(ORDERS):
            if k > 0:
                new = []
                for part in range(2):
                    sums = smooth(now[part], k, lax.rem(d, 2), pair, part)
                    if k == 1:
                        xs = [0.125 * s - x for s, x in zip(sums, now[part])]
                    else:
                        xs = [
                            0.25 * s - (2.0 * x + y)
                            for s, x, y in zip(sums, now[part], before[part])
                        ]
                    new.append(masked(xs) if k < KCHEB else xs)
                before, now = now, new
            for t in range(tiles):
                a = coef[2 * k, t]
                b = coef[2 * k + 1, t]
                p = now[0][t][HALO:HALO + rows]
                q = now[1][t][HALO:HALO + rows]
                if pair == 0:
                    add0, add1 = a * p + b * q, a * q - b * p
                else:
                    add0, add1 = a * p - b * q, a * q + b * p
                total[0][t] = add0 if k == 0 else total[0][t] + add0
                total[1][t] = add1 if k == 0 else total[1][t] + add1
        for part in range(2):
            for t in range(tiles):
                fields[d + 1, 2 * pair + part, t, pl.ds(HALO, rows)] = total[part][t]

    def image_copy(d, source, owner):
        return pltpu.make_async_remote_copy(
            src_ref=partial.at[d],
            dst_ref=arrived.at[d, source],
            send_sem=img_send.at[d],
            recv_sem=img_recv.at[d, source],
            device_id={"freq": owner},
            device_id_type=MESH,
        )

    make_coefficients(0)

    def depth_step(d, carry):
        for pair in range(2):
            wait_halo(d, pair)
            propagate(d, pair)

            @pl.when(d < depths - 1)
            def _():
                send_halo(d + 1, pair)

        for t in range(tiles):
            u = [fields[d + 1, part, t, pl.ds(HALO, rows)] for part in range(4)]
            partial[d, :, t * LANES:(t + 1) * LANES] = u[0] * u[2] + u[1] * u[3]
        owner = d // per

        @pl.when(owner != freq)
        def _():
            image_copy(d, freq, owner).start()

        @pl.when(d < depths - 1)
        def _():
            make_coefficients(d + 1)

        return carry

    lax.fori_loop(0, depths, depth_step, 0)

    for part in range(4):
        for t in range(tiles):
            out_ref[0, part, :, t * LANES:(t + 1) * LANES] = fields[depths, part, t, pl.ds(HALO, rows)]

    for i in range(per):
        d = freq * per + i
        total = partial[d]
        for step in range(1, freqs):
            source = lax.rem(freq + step, freqs)
            image_copy(d, source, source).wait_recv()
            total = total + arrived[d, source]
        image_ref[i] = total

    for d in range(depths):
        for pair in range(2):
            wait_halo_sent(d, pair)
        for step in range(1, freqs):
            vel_copy(d, freq, lax.rem(freq + step, freqs)).wait_send()

        @pl.when(d // per != freq)
        def _():
            image_copy(d, freq, d // per).wait_send()


def body(sizes, wavefields, velocity, filter_table, freq_pick, slab_order):
    lats, freqs = sizes
    depths = slab_order.shape[0]
    _, parts, rows, cols = wavefields.shape
    tiles = cols // LANES
    bins = filter_table.shape[0]
    per = depths // freqs
    table = lax.dynamic_index_in_dim(filter_table, freq_pick[0], 1, keepdims=False)
    table = jnp.transpose(table, (1, 2, 0)).reshape(1, ORDERS * 2 * bins)
    wide = -(-table.shape[1] // LANES) * LANES
    table = jnp.pad(table, ((0, 0), (0, wide - table.shape[1])))
    vmem = pl.BlockSpec(memory_space=pltpu.VMEM)
    return pl.pallas_call(
        functools.partial(kernel, (lats, freqs, bins)),
        out_shape=(
            jax.ShapeDtypeStruct(wavefields.shape, jnp.float32),
            jax.ShapeDtypeStruct((per, rows, cols), jnp.float32),
        ),
        in_specs=[vmem, vmem, vmem, pl.BlockSpec(memory_space=pltpu.SMEM)],
        out_specs=(vmem, vmem),
        scratch_shapes=[
            pltpu.VMEM((depths + 1, parts, tiles + 1, rows + 2 * HALO, LANES), jnp.float32),
            pltpu.VMEM((depths, freqs, rows, cols), jnp.float32),
            pltpu.VMEM((ORDERS * 2, tiles, rows, LANES), jnp.float32),
            pltpu.VMEM((depths, rows, cols), jnp.float32),
            pltpu.VMEM((depths, freqs, rows, cols), jnp.float32),
            pltpu.VMEM((2, parts, tiles + 1, rows + 2 * HALO + 24, LANES), jnp.float32),
            pltpu.SemaphoreType.DMA((depths, 2, 5)),
            pltpu.SemaphoreType.DMA((depths, 2, 5)),
            pltpu.SemaphoreType.DMA((depths, freqs)),
            pltpu.SemaphoreType.DMA((depths, freqs)),
            pltpu.SemaphoreType.DMA((depths,)),
            pltpu.SemaphoreType.DMA((depths, freqs)),
        ],
        compiler_params=pltpu.CompilerParams(
            collective_id=0, has_side_effects=True, vmem_limit_bytes=32 * 1024 * 1024
        ),
    )(wavefields, velocity, table, slab_order)


def solution(mesh):
    sizes = (mesh.shape["lat"], mesh.shape["freq"])
    return jax.shard_map(
        functools.partial(body, sizes),
        mesh=mesh,
        in_specs=(
            P(("shots", "freq"), None, "lat", "sub"),
            P("freq", "lat", "sub"),
            P(),
            P("freq"),
            P(),
        ),
        out_specs=(P(("shots", "freq"), None, "lat", "sub"), P(("shots", "freq"), "lat", "sub")),
        check_vma=False,
    )
```

```python
import functools

import jax
import jax.numpy as jnp
from jax import lax
from jax.experimental import pallas as pl
from jax.experimental.pallas import tpu as pltpu
from jax.sharding import PartitionSpec as P

KCHEB = 8
ORDERS = KCHEB + 1
HALO = 8
LANES = 128
MESH = pl.DeviceIdType.MESH


def kernel(sizes, wave_ref, vel_ref, tab_ref, slab_ref, out_ref, image_ref,
           fields, slots, coef, partial, arrived, tables,
           halo_send, halo_recv, vel_send, vel_recv, img_send, img_recv, *work):
    lats, freqs, bins = sizes
    depths = slab_ref.shape[0]
    slab_size, rows, cols = vel_ref.shape
    tiles = cols // LANES
    per = image_ref.shape[0]
    tall = rows + 2 * HALO
    lat = lax.axis_index("lat")
    sub = lax.axis_index("sub")
    freq = lax.axis_index("freq")
    has_up = lat > 0
    has_down = lat < lats - 1
    other = 1 - sub
    edge_tile = (tiles - 1) * (1 - sub)

    barrier = pltpu.get_barrier_semaphore()

    def greet(target):
        pl.semaphore_signal(barrier, inc=1, device_id=target, device_id_type=MESH)

    greet({"sub": other})
    for step in range(1, freqs):
        greet({"freq": lax.rem(freq + step, freqs)})

    @pl.when(has_up)
    def _():
        greet({"lat": lat - 1})
        greet({"lat": lat - 1, "sub": other})

    @pl.when(has_down)
    def _():
        greet({"lat": lat + 1})
        greet({"lat": lat + 1, "sub": other})

    def vel_copy(d, source, target):
        return pltpu.make_async_remote_copy(
            src_ref=slots.at[d, source],
            dst_ref=slots.at[d, source],
            send_sem=vel_send.at[d, target],
            recv_sem=vel_recv.at[d, source],
            device_id={"freq": target},
            device_id_type=MESH,
        )

    def halo_copy(d, pair, way):
        src_rows = {0: HALO, 1: rows, 2: HALO, 3: HALO, 4: rows}[way]
        dst_rows = {0: HALO + rows, 1: 0, 2: HALO, 3: HALO + rows, 4: 0}[way]
        count = rows if way == 2 else HALO
        src_tiles, dst_tiles = (
            (pl.ds(0, tiles), pl.ds(0, tiles))
            if way < 2
            else (pl.ds(edge_tile, 1), pl.ds(tiles, 1))
        )
        target = {}
        if way in (0, 3):
            target["lat"] = lat - 1
        if way in (1, 4):
            target["lat"] = lat + 1
        if way >= 2:
            target["sub"] = other
        parts = pl.ds(2 * pair, 2)
        return pltpu.make_async_remote_copy(
            src_ref=fields.at[d, parts, src_tiles, pl.ds(src_rows, count)],
            dst_ref=fields.at[d, parts, dst_tiles, pl.ds(dst_rows, count)],
            send_sem=halo_send.at[d, pair, way],
            recv_sem=halo_recv.at[d, pair, way],
            device_id=target,
            device_id_type=MESH,
        )

    def send_halo(d, pair):
        @pl.when(has_up)
        def _():
            halo_copy(d, pair, 0).start()
            halo_copy(d, pair, 3).start()

        @pl.when(has_down)
        def _():
            halo_copy(d, pair, 1).start()
            halo_copy(d, pair, 4).start()

        halo_copy(d, pair, 2).start()

    def wait_halo(d, pair):
        halo_copy(d, pair, 2).wait_recv()

        @pl.when(has_down)
        def _():
            halo_copy(d, pair, 0).wait_recv()
            halo_copy(d, pair, 3).wait_recv()

        @pl.when(has_up)
        def _():
            halo_copy(d, pair, 1).wait_recv()
            halo_copy(d, pair, 4).wait_recv()

    def wait_halo_sent(d, pair):
        @pl.when(has_up)
        def _():
            halo_copy(d, pair, 0).wait_send()
            halo_copy(d, pair, 3).wait_send()

        @pl.when(has_down)
        def _():
            halo_copy(d, pair, 1).wait_send()
            halo_copy(d, pair, 4).wait_send()

        halo_copy(d, pair, 2).wait_send()

    for d in range(depths):
        slots[d, freq] = vel_ref[slab_ref[d] % slab_size]
    for part in range(4):
        for t in range(tiles):
            fields[0, part, t, pl.ds(HALO, rows)] = wave_ref[0, part, :, t * LANES:(t + 1) * LANES]
    pl.semaphore_wait(
        barrier, freqs + jnp.where(has_up, 2, 0) + jnp.where(has_down, 2, 0)
    )

    for step in range(1, freqs):
        vel_copy(0, freq, lax.rem(freq + step, freqs)).start()
    for pair in range(2):
        send_halo(0, pair)
    for d in range(1, depths):
        for step in range(1, freqs):
            vel_copy(d, freq, lax.rem(freq + step, freqs)).start()
    bin_id = lax.broadcasted_iota(jnp.int32, (8, LANES), 1)
    for j in range(ORDERS * 2):
        low = jnp.broadcast_to(tab_ref[j:j + 1], (8, LANES))
        tables[2 * j] = low
        tables[2 * j + 1] = jnp.where(bin_id < bins - 1, pltpu.roll(low, LANES - 1, 1) - low, 0.0)

    lane = lax.broadcasted_iota(jnp.int32, (tall, LANES), 1)
    row = lax.broadcasted_iota(jnp.int32, (tall, LANES), 0)
    row_low = jnp.where(has_up, 0, HALO)
    row_high = jnp.where(has_down, tall, tall - HALO)
    row_mask = (row >= row_low) & (row < row_high)
    lane_low = jnp.where(sub == 0, 0, LANES // 2)
    halo_mask = row_mask & (lane >= lane_low) & (lane < lane_low + LANES // 2)
    first_lane = lane[:8] == 0
    last_lane = lane[:8] == LANES - 1

    def make_coefficients(d):
        for step in range(1, freqs):
            source = lax.rem(freq + step, freqs)
            vel_copy(d, source, source).wait_recv()
        owner = slab_ref[d] // slab_size
        for t in range(tiles):
            for r in range(0, rows, 8):
                v = jnp.zeros((8, LANES), jnp.float32)
                for source in range(freqs):
                    block = slots[d, source, r:r + 8, t * LANES:(t + 1) * LANES]
                    v = jnp.where(owner == source, block, v)
                base = jnp.floor(v)
                upper = v - base
                index = jnp.clip(base.astype(jnp.int32), 0, bins - 1)
                for j in range(ORDERS * 2):
                    low = jnp.take_along_axis(tables[2 * j], index, axis=1, mode="promise_in_bounds")
                    rise = jnp.take_along_axis(tables[2 * j + 1], index, axis=1, mode="promise_in_bounds")
                    coef[j, t, pl.ds(r, 8)] = low + upper * rise

    def kept(x, r, t):
        rows_here = slice(r, r + 8)
        if t == tiles:
            return jnp.where(halo_mask[rows_here], x, 0.0)
        if r < HALO or r >= HALO + rows:
            return jnp.where(row_mask[rows_here], x, 0.0)
        return x

    def propagate(d, pair):
        shift = lax.rem(d, 2) * 8

        def load(k, part, t, r, off=0):
            start = shift + (8 + r + off)
            if off == 0:
                start = pl.multiple_of(start, 8)
            return work[((k % 3) * 2 + part) * (tiles + 1) + t][pl.ds(start, 8)]

        def store(k, part, t, r, x):
            start = pl.multiple_of(shift + (8 + r), 8)
            work[((k % 3) * 2 + part) * (tiles + 1) + t][pl.ds(start, 8)] = x

        blocks = range(0, tall, 8)
        centre = range(HALO, HALO + rows, 8)
        total = [{} for _ in range(2)]

        def add(k, t, r, now):
            a = coef[2 * k, t, r - HALO:r - HALO + 8]
            b = coef[2 * k + 1, t, r - HALO:r - HALO + 8]
            p, q = now
            if pair == 0:
                add0, add1 = a * p + b * q, a * q - b * p
            else:
                add0, add1 = a * p - b * q, a * q + b * p
            total[0][t, r] = add0 if k == 0 else total[0][t, r] + add0
            total[1][t, r] = add1 if k == 0 else total[1][t, r] + add1

        for r in blocks:
            for t in range(tiles + 1):
                now = []
                for part in range(2):
                    x = kept(fields[d, 2 * pair + part, t, r:r + 8], r, t)
                    store(0, part, t, r, x)
                    now.append(x)
                if t < tiles and r in centre:
                    add(0, t, r, now)
        for k in range(1, ORDERS):
            for r in blocks if k < KCHEB else centre:
                new = []
                for part in range(2):
                    xs, ys = [], []
                    for t in range(tiles + 1):
                        x = load(k - 1, part, t, r)
                        above, below = load(k - 1, part, t, r, -1), load(k - 1, part, t, r, 1)
                        twice = x + x
                        xs.append(x if k == 1 else twice)
                        ys.append(above + below + twice)
                    left = [pltpu.roll(y, LANES - 1, 1) for y in ys]
                    right = [pltpu.roll(y, 1, 1) for y in ys]
                    out = []
                    for t in range(tiles + 1 if k < KCHEB else tiles):
                        y = (
                            (ys[t] + ys[t])
                            + jnp.where(last_lane, left[(t + 1) % (tiles + 1)], left[t])
                            + jnp.where(first_lane, right[t - 1], right[t])
                        )
                        if k == 1:
                            z = 0.125 * y - xs[t]
                        else:
                            z = 0.25 * y - (xs[t] + load(k - 2, part, t, r))
                        if k < KCHEB:
                            z = kept(z, r, t)
                            store(k, part, t, r, z)
                        out.append(z)
                    new.append(out)
                if r in centre:
                    for t in range(tiles):
                        add(k, t, r, (new[0][t], new[1][t]))
        for part in range(2):
            for t in range(tiles):
                for r in centre:
                    fields[d + 1, 2 * pair + part, t, r:r + 8] = total[part][t, r]

    def image_copy(d, source, owner):
        return pltpu.make_async_remote_copy(
            src_ref=partial.at[d],
            dst_ref=arrived.at[d, source],
            send_sem=img_send.at[d],
            recv_sem=img_recv.at[d, source],
            device_id={"freq": owner},
            device_id_type=MESH,
        )

    make_coefficients(0)

    def depth_step(d, carry):
        for pair in range(2):
            wait_halo(d, pair)
            propagate(d, pair)

            @pl.when(d < depths - 1)
            def _():
                send_halo(d + 1, pair)

        for t in range(tiles):
            u = [fields[d + 1, part, t, pl.ds(HALO, rows)] for part in range(4)]
            partial[d, :, t * LANES:(t + 1) * LANES] = u[0] * u[2] + u[1] * u[3]
        owner = d // per

        @pl.when(owner != freq)
        def _():
            image_copy(d, freq, owner).start()

        @pl.when(d < depths - 1)
        def _():
            make_coefficients(d + 1)

        return carry

    lax.fori_loop(0, depths, depth_step, 0)

    for part in range(4):
        for t in range(tiles):
            out_ref[0, part, :, t * LANES:(t + 1) * LANES] = fields[depths, part, t, pl.ds(HALO, rows)]

    for i in range(per):
        d = freq * per + i
        total = partial[d]
        for step in range(1, freqs):
            source = lax.rem(freq + step, freqs)
            image_copy(d, source, source).wait_recv()
            total = total + arrived[d, source]
        image_ref[i] = total

    for d in range(depths):
        for pair in range(2):
            wait_halo_sent(d, pair)
        for step in range(1, freqs):
            vel_copy(d, freq, lax.rem(freq + step, freqs)).wait_send()

        @pl.when(d // per != freq)
        def _():
            image_copy(d, freq, d // per).wait_send()


def body(sizes, wavefields, velocity, filter_table, freq_pick, slab_order):
    lats, freqs = sizes
    depths = slab_order.shape[0]
    _, parts, rows, cols = wavefields.shape
    tiles = cols // LANES
    bins = filter_table.shape[0]
    per = depths // freqs
    table = lax.dynamic_index_in_dim(filter_table, freq_pick[0], 1, keepdims=False)
    table = jnp.transpose(table, (1, 2, 0)).reshape(ORDERS * 2, bins)
    table = jnp.pad(table, ((0, 0), (0, LANES - bins)))
    vmem = pl.BlockSpec(memory_space=pltpu.VMEM)
    return pl.pallas_call(
        functools.partial(kernel, (lats, freqs, bins)),
        out_shape=(
            jax.ShapeDtypeStruct(wavefields.shape, jnp.float32),
            jax.ShapeDtypeStruct((per, rows, cols), jnp.float32),
        ),
        in_specs=[vmem, vmem, vmem, pl.BlockSpec(memory_space=pltpu.SMEM)],
        out_specs=(vmem, vmem),
        scratch_shapes=[
            pltpu.VMEM((depths + 1, parts, tiles + 1, rows + 2 * HALO, LANES), jnp.float32),
            pltpu.VMEM((depths, freqs, rows, cols), jnp.float32),
            pltpu.VMEM((ORDERS * 2, tiles, rows, LANES), jnp.float32),
            pltpu.VMEM((depths, rows, cols), jnp.float32),
            pltpu.VMEM((depths, freqs, rows, cols), jnp.float32),
            pltpu.VMEM((ORDERS * 4, 8, LANES), jnp.float32),
            pltpu.SemaphoreType.DMA((depths, 2, 5)),
            pltpu.SemaphoreType.DMA((depths, 2, 5)),
            pltpu.SemaphoreType.DMA((depths, freqs)),
            pltpu.SemaphoreType.DMA((depths, freqs)),
            pltpu.SemaphoreType.DMA((depths,)),
            pltpu.SemaphoreType.DMA((depths, freqs)),
        ]
        + [pltpu.VMEM((rows + 2 * HALO + 24, LANES), jnp.float32)] * (6 * (tiles + 1)),
        compiler_params=pltpu.CompilerParams(
            collective_id=0, has_side_effects=True, vmem_limit_bytes=32 * 1024 * 1024
        ),
    )(wavefields, velocity, table, slab_order)


def solution(mesh):
    sizes = (mesh.shape["lat"], mesh.shape["freq"])
    return jax.shard_map(
        functools.partial(body, sizes),
        mesh=mesh,
        in_specs=(
            P(("shots", "freq"), None, "lat", "sub"),
            P("freq", "lat", "sub"),
            P(),
            P("freq"),
            P(),
        ),
        out_specs=(P(("shots", "freq"), None, "lat", "sub"), P(("shots", "freq"), "lat", "sub")),
        check_vma=False,
    )
```

```python
import functools

import jax
import jax.numpy as jnp
from jax import lax
from jax.experimental import pallas as pl
from jax.experimental.pallas import tpu as pltpu
from jax.sharding import PartitionSpec as P

KCHEB = 8
ORDERS = KCHEB + 1
HALO = 8
LANES = 128
MESH = pl.DeviceIdType.MESH


def kernel(sizes, wave_ref, vel_ref, tab_ref, slab_ref, out_ref, image_ref,
           fields, slots, coef, partial, arrived, spread, stored, load_sem,
           halo_send, halo_recv, vel_send, vel_recv, img_send, img_recv, *work):
    lats, freqs, bins = sizes
    depths = slab_ref.shape[0]
    slab_size, rows, cols = vel_ref.shape
    tiles = cols // LANES
    per = image_ref.shape[0]
    tall = rows + 2 * HALO
    wide = ORDERS * 2 * 8
    chunk = min(256, cols)
    lat = lax.axis_index("lat")
    sub = lax.axis_index("sub")
    freq = lax.axis_index("freq")
    has_up = lat > 0
    has_down = lat < lats - 1
    other = 1 - sub
    edge_tile = (tiles - 1) * (1 - sub)

    barrier = pltpu.get_barrier_semaphore()

    def greet(target):
        pl.semaphore_signal(barrier, inc=1, device_id=target, device_id_type=MESH)

    greet({"sub": other})
    for step in range(1, freqs):
        greet({"freq": lax.rem(freq + step, freqs)})

    @pl.when(has_up)
    def _():
        greet({"lat": lat - 1})
        greet({"lat": lat - 1, "sub": other})

    @pl.when(has_down)
    def _():
        greet({"lat": lat + 1})
        greet({"lat": lat + 1, "sub": other})

    def vel_copy(d, source, target):
        return pltpu.make_async_remote_copy(
            src_ref=slots.at[d, source],
            dst_ref=slots.at[d, source],
            send_sem=vel_send.at[d, target],
            recv_sem=vel_recv.at[d, source],
            device_id={"freq": target},
            device_id_type=MESH,
        )

    def halo_copy(d, pair, way):
        src_rows = {0: HALO, 1: rows, 2: HALO, 3: HALO, 4: rows}[way]
        dst_rows = {0: HALO + rows, 1: 0, 2: HALO, 3: HALO + rows, 4: 0}[way]
        count = rows if way == 2 else HALO
        src_tiles, dst_tiles = (
            (pl.ds(0, tiles), pl.ds(0, tiles))
            if way < 2
            else (pl.ds(edge_tile, 1), pl.ds(tiles, 1))
        )
        target = {}
        if way in (0, 3):
            target["lat"] = lat - 1
        if way in (1, 4):
            target["lat"] = lat + 1
        if way >= 2:
            target["sub"] = other
        parts = pl.ds(2 * pair, 2)
        return pltpu.make_async_remote_copy(
            src_ref=fields.at[d, parts, src_tiles, pl.ds(src_rows, count)],
            dst_ref=fields.at[d, parts, dst_tiles, pl.ds(dst_rows, count)],
            send_sem=halo_send.at[d, pair, way],
            recv_sem=halo_recv.at[d, pair, way],
            device_id=target,
            device_id_type=MESH,
        )

    def send_halo(d, pair):
        @pl.when(has_up)
        def _():
            halo_copy(d, pair, 0).start()
            halo_copy(d, pair, 3).start()

        @pl.when(has_down)
        def _():
            halo_copy(d, pair, 1).start()
            halo_copy(d, pair, 4).start()

        halo_copy(d, pair, 2).start()

    def wait_halo(d, pair):
        halo_copy(d, pair, 2).wait_recv()

        @pl.when(has_down)
        def _():
            halo_copy(d, pair, 0).wait_recv()
            halo_copy(d, pair, 3).wait_recv()

        @pl.when(has_up)
        def _():
            halo_copy(d, pair, 1).wait_recv()
            halo_copy(d, pair, 4).wait_recv()

    def wait_halo_sent(d, pair):
        @pl.when(has_up)
        def _():
            halo_copy(d, pair, 0).wait_send()
            halo_copy(d, pair, 3).wait_send()

        @pl.when(has_down)
        def _():
            halo_copy(d, pair, 1).wait_send()
            halo_copy(d, pair, 4).wait_send()

        halo_copy(d, pair, 2).wait_send()

    loads = [
        pltpu.make_async_copy(
            wave_ref.at[0, :, :, pl.ds(t * LANES, LANES)],
            fields.at[0, :, t, pl.ds(HALO, rows)],
            load_sem.at[t],
        )
        for t in range(tiles)
    ]
    loads.append(pltpu.make_async_copy(vel_ref, stored, load_sem.at[tiles]))
    for copy in loads:
        copy.start()
    for copy in loads:
        copy.wait()
    for d in range(depths):
        slots[d, freq] = stored[slab_ref[d] % slab_size]
    pl.semaphore_wait(
        barrier, freqs + jnp.where(has_up, 2, 0) + jnp.where(has_down, 2, 0)
    )

    for step in range(1, freqs):
        vel_copy(0, freq, lax.rem(freq + step, freqs)).start()
    for pair in range(2):
        send_halo(0, pair)
    for d in range(1, depths):
        for step in range(1, freqs):
            vel_copy(d, freq, lax.rem(freq + step, freqs)).start()
    def one_hot(shape, row_step, col_step):
        i = lax.broadcasted_iota(jnp.int32, shape, 0) // row_step
        j = lax.broadcasted_iota(jnp.int32, shape, 1) // col_step
        return (i == j).astype(jnp.float32)

    tall_table = jnp.dot(
        one_hot((wide, ORDERS * 2), 8, 1), tab_ref[...],
        precision=lax.Precision.HIGHEST, preferred_element_type=jnp.float32,
    )
    full = jnp.dot(
        tall_table, one_hot((bins, bins * 8), 1, 8),
        precision=lax.Precision.HIGHEST, preferred_element_type=jnp.float32,
    )
    same_row = (
        lax.broadcasted_iota(jnp.int32, full.shape, 0) % 8
        == lax.broadcasted_iota(jnp.int32, full.shape, 1) % 8
    )
    full = jnp.where(same_row, full, 0.0)
    high_part = full.astype(jnp.bfloat16)
    spread[:wide] = high_part
    spread[wide:] = (full - high_part.astype(jnp.float32)).astype(jnp.bfloat16)

    lane = lax.broadcasted_iota(jnp.int32, (tall, LANES), 1)
    row = lax.broadcasted_iota(jnp.int32, (tall, LANES), 0)
    row_low = jnp.where(has_up, 0, HALO)
    row_high = jnp.where(has_down, tall, tall - HALO)
    row_mask = (row >= row_low) & (row < row_high)
    lane_low = jnp.where(sub == 0, 0, LANES // 2)
    halo_mask = row_mask & (lane >= lane_low) & (lane < lane_low + LANES // 2)
    first_lane = lane[:8] == 0
    last_lane = lane[:8] == LANES - 1

    def make_coefficients(d):
        for step in range(1, freqs):
            source = lax.rem(freq + step, freqs)
            vel_copy(d, source, source).wait_recv()
        owner = slab_ref[d] // slab_size
        for r in range(0, rows, 8):
            for c in range(0, cols, chunk):
                v = jnp.zeros((8, chunk), jnp.float32)
                for source in range(freqs):
                    v = jnp.where(owner == source, slots[d, source, r:r + 8, c:c + chunk], v)
                hats = jnp.concatenate(
                    [jnp.maximum(0.0, 1.0 - jnp.abs(v - float(i))) for i in range(bins)], axis=0
                )
                high = hats.astype(jnp.bfloat16)
                low = (hats - high.astype(jnp.float32)).astype(jnp.bfloat16)
                both = jnp.dot(spread[...], high, preferred_element_type=jnp.float32)
                rest = jnp.dot(spread[:wide], low, preferred_element_type=jnp.float32)
                out = both[:wide] + (both[wide:] + rest)
                for j in range(ORDERS * 2):
                    for t in range(chunk // LANES):
                        coef[j, c // LANES + t, pl.ds(r, 8)] = out[
                            8 * j:8 * j + 8, t * LANES:(t + 1) * LANES
                        ]

    def kept(x, r, t):
        rows_here = slice(r, r + 8)
        if t == tiles:
            return jnp.where(halo_mask[rows_here], x, 0.0)
        if r < HALO or r >= HALO + rows:
            return jnp.where(row_mask[rows_here], x, 0.0)
        return x

    def propagate(d, pair):
        shift = lax.rem(d, 2) * 8

        def load(k, part, t, r, off=0):
            start = shift + (8 + r + off)
            if off == 0:
                start = pl.multiple_of(start, 8)
            return work[((k % 3) * 2 + part) * (tiles + 1) + t][pl.ds(start, 8)]

        def store(k, part, t, r, x):
            start = pl.multiple_of(shift + (8 + r), 8)
            work[((k % 3) * 2 + part) * (tiles + 1) + t][pl.ds(start, 8)] = x

        blocks = range(0, tall, 8)
        centre = range(HALO, HALO + rows, 8)
        total = [{} for _ in range(2)]

        def add(k, t, r, now):
            a = coef[2 * k, t, r - HALO:r - HALO + 8]
            b = coef[2 * k + 1, t, r - HALO:r - HALO + 8]
            p, q = now
            if pair == 0:
                add0, add1 = a * p + b * q, a * q - b * p
            else:
                add0, add1 = a * p - b * q, a * q + b * p
            total[0][t, r] = add0 if k == 0 else total[0][t, r] + add0
            total[1][t, r] = add1 if k == 0 else total[1][t, r] + add1

        for r in blocks:
            for t in range(tiles + 1):
                now = []
                for part in range(2):
                    x = kept(fields[d, 2 * pair + part, t, r:r + 8], r, t)
                    store(0, part, t, r, x)
                    now.append(x)
                if t < tiles and r in centre:
                    add(0, t, r, now)
        for k in range(1, ORDERS):
            for r in blocks if k < KCHEB else centre:
                new = []
                for part in range(2):
                    xs, ys = [], []
                    for t in range(tiles + 1):
                        x = load(k - 1, part, t, r)
                        above, below = load(k - 1, part, t, r, -1), load(k - 1, part, t, r, 1)
                        twice = x + x
                        xs.append(x if k == 1 else twice)
                        ys.append(above + below + twice)
                    left = [pltpu.roll(y, LANES - 1, 1) for y in ys]
                    right = [pltpu.roll(y, 1, 1) for y in ys]
                    out = []
                    for t in range(tiles + 1 if k < KCHEB else tiles):
                        y = (
                            (ys[t] + ys[t])
                            + jnp.where(last_lane, left[(t + 1) % (tiles + 1)], left[t])
                            + jnp.where(first_lane, right[t - 1], right[t])
                        )
                        if k == 1:
                            z = 0.125 * y - xs[t]
                        else:
                            z = 0.25 * y - (xs[t] + load(k - 2, part, t, r))
                        if k < KCHEB:
                            z = kept(z, r, t)
                            store(k, part, t, r, z)
                        out.append(z)
                    new.append(out)
                if r in centre:
                    for t in range(tiles):
                        add(k, t, r, (new[0][t], new[1][t]))
        for part in range(2):
            for t in range(tiles):
                for r in centre:
                    fields[d + 1, 2 * pair + part, t, r:r + 8] = total[part][t, r]

    def image_copy(d, source, owner):
        return pltpu.make_async_remote_copy(
            src_ref=partial.at[d],
            dst_ref=arrived.at[d, source],
            send_sem=img_send.at[d],
            recv_sem=img_recv.at[d, source],
            device_id={"freq": owner},
            device_id_type=MESH,
        )

    make_coefficients(0)

    def depth_step(d, carry):
        for pair in range(2):
            wait_halo(d, pair)
            propagate(d, pair)

            @pl.when(d < depths - 1)
            def _():
                send_halo(d + 1, pair)

        for t in range(tiles):
            u = [fields[d + 1, part, t, pl.ds(HALO, rows)] for part in range(4)]
            partial[d, :, t * LANES:(t + 1) * LANES] = u[0] * u[2] + u[1] * u[3]
        owner = d // per

        @pl.when(owner != freq)
        def _():
            image_copy(d, freq, owner).start()

        @pl.when(d < depths - 1)
        def _():
            make_coefficients(d + 1)

        return carry

    lax.fori_loop(0, depths, depth_step, 0)

    for part in range(4):
        for t in range(tiles):
            out_ref[0, part, :, t * LANES:(t + 1) * LANES] = fields[depths, part, t, pl.ds(HALO, rows)]

    for i in range(per):
        d = freq * per + i
        total = partial[d]
        for step in range(1, freqs):
            source = lax.rem(freq + step, freqs)
            image_copy(d, source, source).wait_recv()
            total = total + arrived[d, source]
        image_ref[i] = total

    for d in range(depths):
        for pair in range(2):
            wait_halo_sent(d, pair)
        for step in range(1, freqs):
            vel_copy(d, freq, lax.rem(freq + step, freqs)).wait_send()

        @pl.when(d // per != freq)
        def _():
            image_copy(d, freq, d // per).wait_send()


def body(sizes, wavefields, velocity, filter_table, freq_pick, slab_order):
    lats, freqs = sizes
    depths = slab_order.shape[0]
    _, parts, rows, cols = wavefields.shape
    tiles = cols // LANES
    bins = filter_table.shape[0]
    per = depths // freqs
    table = lax.dynamic_index_in_dim(filter_table, freq_pick[0], 1, keepdims=False)
    table = jnp.transpose(table, (1, 2, 0)).reshape(ORDERS * 2, bins)
    vmem = pl.BlockSpec(memory_space=pltpu.VMEM)
    hbm = pl.BlockSpec(memory_space=pltpu.HBM)
    return pl.pallas_call(
        functools.partial(kernel, (lats, freqs, bins)),
        out_shape=(
            jax.ShapeDtypeStruct(wavefields.shape, jnp.float32),
            jax.ShapeDtypeStruct((per, rows, cols), jnp.float32),
        ),
        in_specs=[hbm, hbm, vmem, pl.BlockSpec(memory_space=pltpu.SMEM)],
        out_specs=(vmem, vmem),
        scratch_shapes=[
            pltpu.VMEM((depths + 1, parts, tiles + 1, rows + 2 * HALO, LANES), jnp.float32),
            pltpu.VMEM((depths, freqs, rows, cols), jnp.float32),
            pltpu.VMEM((ORDERS * 2, tiles, rows, LANES), jnp.float32),
            pltpu.VMEM((depths, rows, cols), jnp.float32),
            pltpu.VMEM((depths, freqs, rows, cols), jnp.float32),
            pltpu.VMEM((ORDERS * 2 * 8 * 2, bins * 8), jnp.bfloat16),
            pltpu.VMEM(velocity.shape, jnp.float32),
            pltpu.SemaphoreType.DMA((tiles + 1,)),
            pltpu.SemaphoreType.DMA((depths, 2, 5)),
            pltpu.SemaphoreType.DMA((depths, 2, 5)),
            pltpu.SemaphoreType.DMA((depths, freqs)),
            pltpu.SemaphoreType.DMA((depths, freqs)),
            pltpu.SemaphoreType.DMA((depths,)),
            pltpu.SemaphoreType.DMA((depths, freqs)),
        ]
        + [pltpu.VMEM((rows + 2 * HALO + 24, LANES), jnp.float32)] * (6 * (tiles + 1)),
        compiler_params=pltpu.CompilerParams(
            collective_id=0, has_side_effects=True, vmem_limit_bytes=32 * 1024 * 1024
        ),
    )(wavefields, velocity, table, slab_order)


def solution(mesh):
    sizes = (mesh.shape["lat"], mesh.shape["freq"])
    return jax.shard_map(
        functools.partial(body, sizes),
        mesh=mesh,
        in_specs=(
            P(("shots", "freq"), None, "lat", "sub"),
            P("freq", "lat", "sub"),
            P(),
            P("freq"),
            P(),
        ),
        out_specs=(P(("shots", "freq"), None, "lat", "sub"), P(("shots", "freq"), "lat", "sub")),
        check_vma=False,
    )
```

```python
import functools

import jax
import jax.numpy as jnp
from jax import lax
from jax.experimental import pallas as pl
from jax.experimental.pallas import tpu as pltpu
from jax.sharding import PartitionSpec as P

KCHEB = 8
ORDERS = KCHEB + 1
HALO = 8
WIDE_HALO = 16
LANES = 128
MESH = pl.DeviceIdType.MESH


def kernel(sizes, wave_ref, vel_ref, tab_ref, slab_ref, out_ref, image_ref,
           fields, middle, slots, coef_first, coef_second, partial, arrived, spread, stored, load_sem,
           halo_send, halo_recv, vel_send, vel_recv, img_send, img_recv, *work):
    lats, freqs, bins = sizes
    depths = slab_ref.shape[0]
    slab_size, rows, cols = vel_ref.shape
    tiles = cols // LANES
    per = image_ref.shape[0]
    rounds = depths // 2
    wide = ORDERS * 2 * 8
    lat = lax.axis_index("lat")
    sub = lax.axis_index("sub")
    freq = lax.axis_index("freq")
    has_up = lat > 0
    has_down = lat < lats - 1
    other = 1 - sub
    edge_tile = (tiles - 1) * (1 - sub)

    barrier = pltpu.get_barrier_semaphore()

    def greet_row(target):
        for step in range(freqs):
            place = dict(target, freq=lax.rem(freq + step, freqs))
            if step > 0 or target:
                pl.semaphore_signal(barrier, inc=1, device_id=place, device_id_type=MESH)
            pl.semaphore_signal(
                barrier, inc=1, device_id=dict(place, sub=other), device_id_type=MESH
            )

    greet_row({})

    @pl.when(has_up)
    def _():
        greet_row({"lat": lat - 1})

    @pl.when(has_down)
    def _():
        greet_row({"lat": lat + 1})

    loads = [
        pltpu.make_async_copy(
            wave_ref.at[0, :, :, pl.ds(t * LANES, LANES)],
            fields.at[0, :, t, pl.ds(WIDE_HALO, rows)],
            load_sem.at[t],
        )
        for t in range(tiles)
    ]
    loads.append(pltpu.make_async_copy(vel_ref, stored, load_sem.at[tiles]))
    for copy in loads:
        copy.start()
    for copy in loads:
        copy.wait()
    for d in range(depths):
        row_here = stored[slab_ref[d] % slab_size]
        for t in range(tiles):
            slots[d, freq, t, pl.ds(HALO, rows)] = row_here[:, t * LANES:(t + 1) * LANES]
    pl.semaphore_wait(
        barrier, 2 * freqs * (1 + jnp.where(has_up, 1, 0) + jnp.where(has_down, 1, 0)) - 1
    )

    def place_of(way, halo):
        src_rows = (halo, rows, halo, halo, rows, halo)[way]
        dst_rows = (halo + rows, 0, halo, halo + rows, 0, halo)[way]
        count = rows if way in (2, 5) else halo
        if way in (0, 1, 5):
            src_tiles, dst_tiles = pl.ds(0, tiles), pl.ds(0, tiles)
        else:
            src_tiles, dst_tiles = pl.ds(edge_tile, 1), pl.ds(tiles, 1)
        target = {}
        if way in (0, 3):
            target["lat"] = lat - 1
        if way in (1, 4):
            target["lat"] = lat + 1
        if way in (2, 3, 4):
            target["sub"] = other
        return (src_tiles, pl.ds(src_rows, count)), (dst_tiles, pl.ds(dst_rows, count)), target

    def vel_copy(d, source, target, way):
        src, dst, place = place_of(way, HALO)
        return pltpu.make_async_remote_copy(
            src_ref=slots.at[d, source, *src],
            dst_ref=slots.at[d, source, *dst],
            send_sem=vel_send.at[d, target, way],
            recv_sem=vel_recv.at[d, source, way],
            device_id=dict(place, freq=target),
            device_id_type=MESH,
        )

    def halo_copy(e, pair, way):
        src, dst, place = place_of(way, WIDE_HALO)
        parts = pl.ds(2 * pair, 2)
        return pltpu.make_async_remote_copy(
            src_ref=fields.at[e, parts, *src],
            dst_ref=fields.at[e, parts, *dst],
            send_sem=halo_send.at[e, pair, way],
            recv_sem=halo_recv.at[e, pair, way],
            device_id=place,
            device_id_type=MESH,
        )

    def all_ways(do):
        @pl.when(has_up)
        def _():
            do(0)
            do(3)

        @pl.when(has_down)
        def _():
            do(1)
            do(4)

        do(2)

    def all_ways_in(do):
        @pl.when(has_down)
        def _():
            do(0)
            do(3)

        @pl.when(has_up)
        def _():
            do(1)
            do(4)

        do(2)

    def each_velocity(d, do):
        for step in range(freqs):
            target = lax.rem(freq + step, freqs)
            if step > 0:
                do(vel_copy(d, freq, target, 5))
            if d % 2 == 0:
                all_ways(lambda way: do(vel_copy(d, freq, target, way)))

    def send_halo(e, pair):
        all_ways(lambda way: halo_copy(e, pair, way).start())

    def wait_halo(e, pair):
        all_ways_in(lambda way: halo_copy(e, pair, way).wait_recv())

    each_velocity(0, lambda copy: copy.start())
    for pair in range(2):
        send_halo(0, pair)
    for d in range(1, depths):
        each_velocity(d, lambda copy: copy.start())
    def one_hot(shape, row_step, col_step):
        i = lax.broadcasted_iota(jnp.int32, shape, 0) // row_step
        j = lax.broadcasted_iota(jnp.int32, shape, 1) // col_step
        return (i == j).astype(jnp.float32)

    tall_table = jnp.dot(
        one_hot((wide, ORDERS * 2), 8, 1), tab_ref[...],
        precision=lax.Precision.HIGHEST, preferred_element_type=jnp.float32,
    )
    full = jnp.dot(
        tall_table, one_hot((bins, bins * 8), 1, 8),
        precision=lax.Precision.HIGHEST, preferred_element_type=jnp.float32,
    )
    same_row = (
        lax.broadcasted_iota(jnp.int32, full.shape, 0) % 8
        == lax.broadcasted_iota(jnp.int32, full.shape, 1) % 8
    )
    full = jnp.where(same_row, full, 0.0)
    high_part = full.astype(jnp.bfloat16)
    spread[:wide] = high_part
    spread[wide:] = (full - high_part.astype(jnp.float32)).astype(jnp.bfloat16)

    lane = lax.broadcasted_iota(jnp.int32, (8, LANES), 1)
    lane_low = jnp.where(sub == 0, 0, LANES // 2)
    side = (lane >= lane_low) & (lane < lane_low + LANES // 2)
    everywhere = lane >= 0
    above = everywhere & (jnp.where(has_up, 1, 0) > 0)
    below = everywhere & (jnp.where(has_down, 1, 0) > 0)
    first_lane = lane == 0
    last_lane = lane == LANES - 1

    def make_coefficients(d, first):
        coef = coef_first if first else coef_second
        owner = slab_ref[d] // slab_size
        blocks = range(0, rows + 2 * HALO, 8) if first else range(HALO, HALO + rows, 8)
        for r in blocks:
            for t0 in range(0, tiles + 1 if first else tiles, 2):
                pieces = range(t0, min(t0 + 2, tiles + 1 if first else tiles))
                views = []
                for t in pieces:
                    v = jnp.zeros((8, LANES), jnp.float32)
                    for source in range(freqs):
                        v = jnp.where(owner == source, slots[d, source, t, r:r + 8], v)
                    views.append(v)
                v = jnp.concatenate(views, axis=1)
                hats = jnp.concatenate(
                    [jnp.maximum(0.0, 1.0 - jnp.abs(v - float(i))) for i in range(bins)], axis=0
                )
                high = hats.astype(jnp.bfloat16)
                low = (hats - high.astype(jnp.float32)).astype(jnp.bfloat16)
                both = jnp.dot(spread[...], high, preferred_element_type=jnp.float32)
                rest = jnp.dot(spread[:wide], low, preferred_element_type=jnp.float32)
                out = both[:wide] + (both[wide:] + rest)
                for j in range(ORDERS * 2):
                    for t in pieces:
                        coef[j, t, pl.ds(r, 8)] = out[
                            8 * j:8 * j + 8, (t - t0) * LANES:(t - t0 + 1) * LANES
                        ]

    def wait_velocity(d, first):
        for step in range(freqs):
            source = lax.rem(freq + step, freqs)
            if step > 0:
                vel_copy(d, source, source, 5).wait_recv()
            if first:
                all_ways_in(lambda way: vel_copy(d, source, source, way).wait_recv())

    def propagate(e, pair, first):
        shift = lax.rem(e, 2) * 8
        halo = WIDE_HALO if first else HALO
        tall = rows + 2 * halo
        out_tiles = tiles + 1 if first else tiles
        coef = coef_first if first else coef_second
        coef_row = 0 if first else HALO

        def kept(x, r, t):
            inside = side if t == tiles else None
            if r < halo:
                inside = above if inside is None else inside & above
            if r >= halo + rows:
                inside = below if inside is None else inside & below
            return x if inside is None else jnp.where(inside, x, 0.0)

        def load(k, part, t, r, off=0):
            start = shift + (8 + r + off)
            if off == 0:
                start = pl.multiple_of(start, 8)
            return work[((k % 3) * 2 + part) * (tiles + 1) + t][pl.ds(start, 8)]

        def store(k, part, t, r, x):
            start = pl.multiple_of(shift + (8 + r), 8)
            work[((k % 3) * 2 + part) * (tiles + 1) + t][pl.ds(start, 8)] = x

        blocks = range(0, tall, 8)
        centre = range(HALO, tall - HALO, 8)
        total = [{} for _ in range(2)]

        def add(k, t, r, now):
            a = coef[2 * k, t, pl.ds(r - HALO + coef_row, 8)]
            b = coef[2 * k + 1, t, pl.ds(r - HALO + coef_row, 8)]
            p, q = now
            if pair == 0:
                add0, add1 = a * p + b * q, a * q - b * p
            else:
                add0, add1 = a * p - b * q, a * q + b * p
            total[0][t, r] = add0 if k == 0 else total[0][t, r] + add0
            total[1][t, r] = add1 if k == 0 else total[1][t, r] + add1

        for r in blocks:
            for t in range(tiles + 1):
                now = []
                for part in range(2):
                    if first:
                        x = fields[e, 2 * pair + part, t, r:r + 8]
                    else:
                        x = middle[2 * pair + part, t, r:r + 8]
                    x = kept(x, r, t)
                    store(0, part, t, r, x)
                    now.append(x)
                if t < out_tiles and r in centre:
                    add(0, t, r, now)
        for k in range(1, ORDERS):
            for r in blocks if k < KCHEB else centre:
                new = []
                for part in range(2):
                    xs, ys = [], []
                    for t in range(tiles + 1):
                        x = load(k - 1, part, t, r)
                        upper, lower = load(k - 1, part, t, r, -1), load(k - 1, part, t, r, 1)
                        twice = x + x
                        xs.append(x if k == 1 else twice)
                        ys.append(upper + lower + twice)
                    left = [pltpu.roll(y, LANES - 1, 1) for y in ys]
                    right = [pltpu.roll(y, 1, 1) for y in ys]
                    out = []
                    for t in range(tiles + 1 if k < KCHEB else out_tiles):
                        y = (
                            (ys[t] + ys[t])
                            + jnp.where(last_lane, left[(t + 1) % (tiles + 1)], left[t])
                            + jnp.where(first_lane, right[t - 1], right[t])
                        )
                        if k == 1:
                            z = 0.125 * y - xs[t]
                        else:
                            z = 0.25 * y - (xs[t] + load(k - 2, part, t, r))
                        if k < KCHEB:
                            z = kept(z, r, t)
                            store(k, part, t, r, z)
                        out.append(z)
                    new.append(out)
                if r in centre:
                    for t in range(out_tiles):
                        add(k, t, r, (new[0][t], new[1][t]))
        for part in range(2):
            for t in range(out_tiles):
                for r in centre:
                    if first:
                        middle[2 * pair + part, t, pl.ds(r - HALO, 8)] = total[part][t, r]
                    else:
                        fields[e + 1, 2 * pair + part, t, pl.ds(r + HALO, 8)] = total[part][t, r]

    def image_copy(d, source, owner):
        return pltpu.make_async_remote_copy(
            src_ref=partial.at[d],
            dst_ref=arrived.at[d, source],
            send_sem=img_send.at[d],
            recv_sem=img_recv.at[d, source],
            device_id={"freq": owner},
            device_id_type=MESH,
        )

    def coefficients_of(e):
        for first in (True, False):
            wait_velocity(2 * e + (0 if first else 1), first)
            make_coefficients(2 * e + (0 if first else 1), first)

    def make_image(d, cells):
        for t in range(tiles):
            u = [cells(part, t) for part in range(4)]
            partial[d, :, t * LANES:(t + 1) * LANES] = u[0] * u[2] + u[1] * u[3]
        owner = d // per

        @pl.when(owner != freq)
        def _():
            image_copy(d, freq, owner).start()

    coefficients_of(0)

    def round_step(e, carry):
        for pair in range(2):
            wait_halo(e, pair)
            propagate(e, pair, True)
            propagate(e, pair, False)

            @pl.when(e < rounds - 1)
            def _():
                send_halo(e + 1, pair)

        make_image(2 * e, lambda part, t: middle[part, t, pl.ds(HALO, rows)])
        make_image(2 * e + 1, lambda part, t: fields[e + 1, part, t, pl.ds(WIDE_HALO, rows)])

        @pl.when(e < rounds - 1)
        def _():
            coefficients_of(e + 1)

        return carry

    lax.fori_loop(0, rounds, round_step, 0)

    for part in range(4):
        for t in range(tiles):
            out_ref[0, part, :, t * LANES:(t + 1) * LANES] = fields[rounds, part, t, pl.ds(WIDE_HALO, rows)]

    for i in range(per):
        d = freq * per + i
        total = partial[d]
        for step in range(1, freqs):
            source = lax.rem(freq + step, freqs)
            image_copy(d, source, source).wait_recv()
            total = total + arrived[d, source]
        image_ref[i] = total

    for e in range(rounds):
        for pair in range(2):
            all_ways(lambda way: halo_copy(e, pair, way).wait_send())
    for d in range(depths):
        each_velocity(d, lambda copy: copy.wait_send())

        @pl.when(d // per != freq)
        def _():
            image_copy(d, freq, d // per).wait_send()


def body(sizes, wavefields, velocity, filter_table, freq_pick, slab_order):
    lats, freqs = sizes
    depths = slab_order.shape[0]
    _, parts, rows, cols = wavefields.shape
    tiles = cols // LANES
    bins = filter_table.shape[0]
    per = depths // freqs
    rounds = depths // 2
    table = lax.dynamic_index_in_dim(filter_table, freq_pick[0], 1, keepdims=False)
    table = jnp.transpose(table, (1, 2, 0)).reshape(ORDERS * 2, bins)
    vmem = pl.BlockSpec(memory_space=pltpu.VMEM)
    hbm = pl.BlockSpec(memory_space=pltpu.HBM)
    return pl.pallas_call(
        functools.partial(kernel, (lats, freqs, bins)),
        out_shape=(
            jax.ShapeDtypeStruct(wavefields.shape, jnp.float32),
            jax.ShapeDtypeStruct((per, rows, cols), jnp.float32),
        ),
        in_specs=[hbm, hbm, vmem, pl.BlockSpec(memory_space=pltpu.SMEM)],
        out_specs=(vmem, vmem),
        scratch_shapes=[
            pltpu.VMEM((rounds + 1, parts, tiles + 1, rows + 2 * WIDE_HALO, LANES), jnp.float32),
            pltpu.VMEM((parts, tiles + 1, rows + 2 * HALO, LANES), jnp.float32),
            pltpu.VMEM((depths, freqs, tiles + 1, rows + 2 * HALO, LANES), jnp.float32),
            pltpu.VMEM((ORDERS * 2, tiles + 1, rows + 2 * HALO, LANES), jnp.float32),
            pltpu.VMEM((ORDERS * 2, tiles + 1, rows + 2 * HALO, LANES), jnp.float32),
            pltpu.VMEM((depths, rows, cols), jnp.float32),
            pltpu.VMEM((depths, freqs, rows, cols), jnp.float32),
            pltpu.VMEM((ORDERS * 2 * 8 * 2, bins * 8), jnp.bfloat16),
            pltpu.VMEM(velocity.shape, jnp.float32),
            pltpu.SemaphoreType.DMA((tiles + 1,)),
            pltpu.SemaphoreType.DMA((rounds, 2, 5)),
            pltpu.SemaphoreType.DMA((rounds, 2, 5)),
            pltpu.SemaphoreType.DMA((depths, freqs, 6)),
            pltpu.SemaphoreType.DMA((depths, freqs, 6)),
            pltpu.SemaphoreType.DMA((depths,)),
            pltpu.SemaphoreType.DMA((depths, freqs)),
        ]
        + [pltpu.VMEM((rows + 2 * WIDE_HALO + 24, LANES), jnp.float32)] * (6 * (tiles + 1)),
        compiler_params=pltpu.CompilerParams(
            collective_id=0, has_side_effects=True, vmem_limit_bytes=56 * 1024 * 1024
        ),
    )(wavefields, velocity, table, slab_order)


def solution(mesh):
    sizes = (mesh.shape["lat"], mesh.shape["freq"])
    return jax.shard_map(
        functools.partial(body, sizes),
        mesh=mesh,
        in_specs=(
            P(("shots", "freq"), None, "lat", "sub"),
            P("freq", "lat", "sub"),
            P(),
            P("freq"),
            P(),
        ),
        out_specs=(P(("shots", "freq"), None, "lat", "sub"), P(("shots", "freq"), "lat", "sub")),
        check_vma=False,
    )
```
